32 devices in a mesh: src: 8 (over z, x), att: 4 (over y, core).
Axes of the slice: x: 2, y: 2, z: 4, core: 2. Of those that a mesh axis runs over, the one named last changes fastest.
Arguments:
- residual: float32 [262144], P(('src', 'att')), may hold values from -6 to 6
- weight: float32 [262144], P(('src', 'att')), may hold values from 0.2 to 5
- source_part: float32 [5, 262144], P(None, ('src', 'att')), may hold values from -6 to 6
- attitude_part: float32 [4, 262144], P(None, ('src', 'att')), may hold values from -6 to 6
- calib_part: float32 [262144], P(('src', 'att')), may hold values from -6 to 6
- phase: float32 [262144], P(('src', 'att')), may hold values from 0 to 1
- obs_source: int32 [262144], P(('src', 'att')), may hold values from 0 to 63
- obs_owner: int32 [262144], P(('src', 'att')), may hold values from 0 to 31
- obs_slot: int32 [262144], P(('src', 'att')), may hold values from 0 to 3
- obs_knot: int32 [262144], P(('src', 'att')), may hold values from 0 to 124
- obs_calib: int32 [262144], P(('src', 'att')), may hold values from 0 to 2047
- tile_count: int32 [32, 4], P(('src', 'att')), may hold values from 1 to 2048, 5120 in all within a row
- time_list: int32 [32, 32, 4], P(None, ('src', 'att')), may hold values from 0 to 7
Outputs:
- source_update: float32 [5, 8192], P(None, ('src', 'att'))
- attitude_update: float32 [4, 32768], P(None, ('src', 'att'))
- calib_update: float32 [2048], replicated
- residual_out: float32 [262144], P(('src', 'att'))
The draws below stay inside these ranges and needn't reach their ends.
Inputs may be any that keep to these rules, and one draw needn't show every extreme that they name: `tile_count`: each device's tile counts sum to 5120. `time_list`: local knot block of the owner; entries may repeat.
All inputs are finite; a program needn't handle non-finite values.
Results may differ from the reference program's by a relative error of at most 0.0001.
Values sent between devices are 32-bit elements; how exact they have to be, the bound alone decides.
A program may use at most 64 MiB of HBM per device.

```python
import math
import jax
import jax.numpy as jnp
import numpy as np

TILES_DEV = 4
OBS_TILE = 2048
SRC_TILE = 64
KNOT = 128
LIST = 4
KB_DEV = 8
NCAL = 2048
OBS_DEV = 8192
LIVE_DEV = 5120
OBS = 262144
SOURCES = 8192
KNOTS = 32768
DEVICES = 32


def plant(values, own_key, low, largest):
    place = [jax.random.randint(jax.random.fold_in(own_key, axis), (), 0, length) for axis, length in enumerate(values.shape)]
    main_axis = values.shape.index(max(values.shape))
    neighbour = place[:main_axis] + [(place[main_axis] + 1) % values.shape[main_axis]] + place[main_axis + 1:]
    return values.at[tuple(place)].set(low).at[tuple(neighbour)].set(largest)


def levels(own_key, dims, pieces, least, high):
    def one(position, blocks):
        heights = jax.random.uniform(jax.random.fold_in(jax.random.fold_in(own_key, 6), position), (blocks,), jnp.float32, least / len(pieces), high / len(pieces))
        return jnp.repeat(jnp.exp(heights), dims[position] // blocks).reshape((-1,) + (1,) * (len(dims) - position - 1))

    factor_of = one(*pieces[0])
    for cut in pieces[1:]:
        factor_of = factor_of * one(*cut)
    return factor_of


def length_profile(count, total, reach, lean):
    weights = [(1 << 20) // math.isqrt(standing ** lean) + 1 for standing in range(2, count + 1)]
    surplus, given = total - reach - (count - 1), [1] * (count - 1)
    while surplus > 0:
        movable = [i for i in range(count - 1) if given[i] < reach]
        mass, budget = sum([weights[i] for i in movable]), surplus
        for i in movable:
            more = min(reach - given[i], max(1, budget * weights[i] // mass), surplus)
            given[i] = given[i] + more
            surplus = surplus - more
    return np.array([reach] + given)


def ragged(rng, amount, total, most, lean):
    if amount == 2:
        one = jax.random.randint(rng, (), max(1, total - most), min(most, total - 1) + 1)
        return jnp.stack([one, total - one])
    tallies = jnp.asarray(length_profile(amount, total, most, lean), jnp.int32)
    pairs = (amount - 1) // 2
    source_of, receiver = tallies[1:1 + 2 * pairs:2], tallies[2:2 + 2 * pairs:2]
    margin = jnp.minimum(source_of - 1, most - receiver)
    shifted = jax.random.randint(jax.random.fold_in(rng, 1), (pairs,), 0, 1 << 20) % (margin + 1)
    tallies = tallies.at[1:1 + 2 * pairs:2].set(source_of - shifted).at[2:2 + 2 * pairs:2].set(receiver + shifted)
    return tallies[jax.random.permutation(jax.random.fold_in(rng, 2), amount)]


def noise(rng, dims, width, bound, shards=(), kind=jnp.bfloat16):
    loudness = levels(rng, dims, shards, -0.22, 0.18) if shards else 1.0
    drawn = jax.random.normal(rng, dims, jnp.float32) * width * loudness
    return jnp.minimum(jnp.maximum(drawn, -bound), bound).astype(kind)


def setup_inputs(seed: int = 0) -> dict:
    arg_keys = jax.random.split(jax.random.key(seed), 14)
    residual = noise(arg_keys[0], (OBS,), 1.0, 6.0, ((0, 32),), jnp.float32)
    weight = jnp.clip(jnp.exp(math.log(5.0) - 3.218876 * jax.random.uniform(arg_keys[1], (OBS,), jnp.float32) ** levels(arg_keys[1], (OBS,), ((0, 32),), -0.2, 0.2)), 0.2, 5.0)
    source_part = noise(arg_keys[2], (5, OBS), 1.0, 6.0, ((1, 32),), jnp.float32)
    attitude_part = noise(arg_keys[3], (4, OBS), 1.0, 6.0, ((1, 32),), jnp.float32)
    calib_part = noise(arg_keys[4], (OBS,), 1.0, 6.0, ((0, 32),), jnp.float32)
    phase = jnp.clip(1.0 * jax.random.uniform(arg_keys[5], (OBS,), jnp.float32) ** levels(arg_keys[5], (OBS,), ((0, 32),), -0.2, 0.2), 0.0, 1.0)
    obs_source = plant(jax.random.randint(arg_keys[6], (OBS,), 0, SRC_TILE), jax.random.fold_in(arg_keys[6], 1), 0, SRC_TILE - 1).astype(jnp.int32)
    obs_owner = plant(jax.random.randint(arg_keys[7], (OBS,), 0, DEVICES), jax.random.fold_in(arg_keys[7], 1), 0, DEVICES - 1).astype(jnp.int32)
    obs_slot = plant(jax.random.randint(arg_keys[8], (OBS,), 0, LIST), jax.random.fold_in(arg_keys[8], 1), 0, LIST - 1).astype(jnp.int32)
    obs_knot = plant(jax.random.randint(arg_keys[9], (OBS,), 0, KNOT - 3), jax.random.fold_in(arg_keys[9], 1), 0, (KNOT - 3) - 1).astype(jnp.int32)
    obs_calib = plant(jax.random.randint(arg_keys[10], (OBS,), 0, NCAL), jax.random.fold_in(arg_keys[10], 1), 0, NCAL - 1).astype(jnp.int32)
    tile_count = jax.vmap(lambda own: ragged(own, TILES_DEV, LIVE_DEV, OBS_TILE, 2))(jax.random.split(arg_keys[11], DEVICES)).reshape((DEVICES, TILES_DEV)).astype(jnp.int32)
    time_list = plant(jax.random.randint(arg_keys[12], (DEVICES, DEVICES, LIST), 0, KB_DEV), jax.random.fold_in(arg_keys[12], 1), 0, KB_DEV - 1).astype(jnp.int32)
    return {"residual": residual, "weight": weight, "source_part": source_part, "attitude_part": attitude_part, "calib_part": calib_part, "phase": phase, "obs_source": obs_source, "obs_owner": obs_owner, "obs_slot": obs_slot, "obs_knot": obs_knot, "obs_calib": obs_calib, "tile_count": tile_count, "time_list": time_list}


def spline_weights(phase):
    other = 1.0 - phase
    square = phase * phase
    cube = square * phase
    return [other * other * other / 6.0, (3.0 * cube - 6.0 * square + 4.0) / 6.0,
            (-3.0 * cube + 3.0 * square + 3.0 * phase + 1.0) / 6.0, cube / 6.0]


def solve_normals(sums):
    matrix = [[None] * 5 for _ in range(5)]
    column = 0
    for left in range(5):
        for right in range(left, 5):
            matrix[left][right] = sums[:, column]
            matrix[right][left] = sums[:, column]
            column += 1
    target = [sums[:, 15 + left] for left in range(5)]
    for left in range(5):
        matrix[left][left] = matrix[left][left] + 1.0
    for pivot in range(5):
        for lower in range(pivot + 1, 5):
            factor = matrix[lower][pivot] / matrix[pivot][pivot]
            for right in range(pivot, 5):
                matrix[lower][right] = matrix[lower][right] - factor * matrix[pivot][right]
            target[lower] = target[lower] - factor * target[pivot]
    result = [None] * 5
    for pivot in range(4, -1, -1):
        value = target[pivot]
        for right in range(pivot + 1, 5):
            value = value - matrix[pivot][right] * result[right]
        result[pivot] = value / matrix[pivot][pivot]
    return jnp.stack(result, 0)


def reference(residual, weight, source_part, attitude_part, calib_part, phase, obs_source, obs_owner, obs_slot, obs_knot, obs_calib, tile_count, time_list):
    index = jnp.arange(OBS, dtype=jnp.int32)
    tile = index // OBS_TILE
    device = index // OBS_DEV
    live = (index % OBS_TILE) < tile_count.reshape(-1)[tile]
    weighted = jnp.where(live, weight, jnp.float32(0.0))
    source = tile * SRC_TILE + obs_source
    columns = []
    for left in range(5):
        for right in range(left, 5):
            columns.append(weighted * source_part[left] * source_part[right])
    for left in range(5):
        columns.append(weighted * source_part[left] * residual)
    sums = jax.ops.segment_sum(jnp.stack(columns, 1), source, num_segments=SOURCES)
    source_update = solve_normals(sums)
    first = residual - jnp.sum(source_part * source_update[:, source], axis=0)
    basis = spline_weights(phase)
    block = obs_owner * KB_DEV + time_list[device, obs_owner, obs_slot]
    knot_base = block * KNOT + obs_knot
    rhs = jnp.zeros((KNOTS, 4), jnp.float32)
    diag = jnp.zeros((KNOTS, 4), jnp.float32)
    for offset in range(4):
        spread = basis[offset][:, None] * attitude_part.T
        rhs = rhs + jax.ops.segment_sum(weighted[:, None] * spread * first[:, None], knot_base + offset, num_segments=KNOTS)
        diag = diag + jax.ops.segment_sum(weighted[:, None] * spread * spread, knot_base + offset, num_segments=KNOTS)
    update = rhs / (diag + 1.0)
    crhs = jax.ops.segment_sum(weighted * calib_part * first, obs_calib, num_segments=NCAL)
    cdiag = jax.ops.segment_sum(weighted * calib_part * calib_part, obs_calib, num_segments=NCAL)
    calib_update = crhs / (cdiag + 1.0)
    correction = jnp.zeros_like(first)
    for offset in range(4):
        correction = correction + basis[offset] * jnp.sum(attitude_part.T * update[knot_base + offset], axis=1)
    residual_out = first - correction - calib_part * calib_update[obs_calib]
    return source_update, update.T, calib_update, residual_out
```

```python
import functools

import jax
import jax.numpy as jnp
from jax import lax
from jax.experimental import pallas as pl
from jax.experimental.pallas import tpu as pltpu
from jax.sharding import PartitionSpec as P

OBS_TILE = 2048
SRC_TILE = 64
KNOT = 128
LIST = 4
KB_DEV = 8
NCAL = 2048

HALF = 64
WIN = 72
LO = 64
CHUNK = 1024
F32 = jnp.float32
BF16 = jnp.bfloat16
NT = (((1,), (1,)), ((), ()))
NN = (((1,), (0,)), ((), ()))


def mm(left, right, dims):
    return lax.dot_general(left, right, dims, preferred_element_type=F32)


def split2(value):
    high = value.astype(BF16)
    low = (value - high.astype(F32)).astype(BF16)
    return high, low


def split3(value):
    high = value.astype(BF16)
    rest = value - high.astype(F32)
    middle = rest.astype(BF16)
    low = (rest - middle.astype(F32)).astype(BF16)
    return high, middle, low


def hot(rows, index):
    count = index.shape[1]
    match = lax.broadcasted_iota(jnp.int32, (rows, count), 0) == index
    return jnp.where(match, F32(1.0), F32(0.0)).astype(BF16)


def kernel(
    devices,
    n_att,
    count_ref,
    residual,
    weight,
    source_part,
    attitude_part,
    calib_part,
    phase,
    obs_source,
    obs_owner,
    obs_slot,
    obs_knot,
    obs_calib,
    list_row,
    list_col,
    source_out,
    attitude_out,
    calib_out,
    residual_out,
    sel,
    lin_all,
    first_all,
    weighted_all,
    calhot,
    srchot,
    acc,
    acc_cal,
    cdiag_keep,
    send_diag,
    send_rhs,
    recv_diag,
    recv_rhs,
    send_ret,
    recv_ret,
    send_cal,
    recv_cal,
    send_calret,
    recv_calret,
    send_sem,
    recv_sem,
):
    rows_a = devices * LIST * 2
    count = residual.shape[1]
    tiles = count // OBS_TILE
    share = NCAL // devices
    me_src = lax.axis_index("src")
    me_att = lax.axis_index("att")
    me = me_src * n_att + me_att

    def peer_of(step):
        peer = lax.rem(me + step, devices)
        return peer, (peer // n_att, lax.rem(peer, n_att))

    barrier = pltpu.get_barrier_semaphore()

    def greet(step, carry):
        _, where = peer_of(step)
        pl.semaphore_signal(
            barrier, inc=1, device_id=where, device_id_type=pl.DeviceIdType.MESH
        )
        return carry

    lax.fori_loop(1, devices, greet, 0)

    def spread(source, target, which):
        def one(step, carry):
            peer, where = peer_of(step)
            pltpu.make_async_remote_copy(
                src_ref=source.at[peer],
                dst_ref=target.at[me],
                send_sem=send_sem.at[which],
                recv_sem=recv_sem.at[which],
                device_id=where,
                device_id_type=pl.DeviceIdType.MESH,
            ).start()
            return carry

        pltpu.make_async_copy(source.at[me], target.at[me], recv_sem.at[which]).start()
        lax.fori_loop(1, devices, one, 0)

    def arrive(target, which):
        pltpu.make_async_copy(target, target, recv_sem.at[which]).wait()

    def left(source, which):
        part = source.at[pl.ds(0, devices - 1)]
        pltpu.make_async_copy(part, part, send_sem.at[which]).wait()

    def packed(sums):
        odd = lax.rem(lax.broadcasted_iota(jnp.int32, (8, rows_a), 1), 2) == 1
        pieces = []
        for c in range(4):
            block = sums[c * WIN : (c + 1) * WIN]
            over = pltpu.roll(block[HALF:WIN], 1, 1)
            pieces.append(block[0:8] + jnp.where(odd, over, F32(0.0)))
            pieces.append(block[8:HALF])
        return jnp.concatenate(pieces, 0).T

    acc[...] = jnp.zeros_like(acc)
    acc_cal[...] = jnp.zeros_like(acc_cal)
    per_tile = OBS_TILE // CHUNK

    def diag_step(step, carry):
        here = pl.ds(pl.multiple_of(step * CHUNK, CHUNK), CHUNK)
        tile = step // per_tile
        place = lax.broadcasted_iota(jnp.int32, (1, CHUNK), 1) + (step - tile * per_tile) * CHUNK
        weighted = jnp.where(place < count_ref[0, tile], weight[:, here], F32(0.0))
        weighted_all[:, here] = weighted
        u = phase[:, here]
        other = 1.0 - u
        square = u * u
        cube = square * u
        b0 = other * other * other / 6.0
        b1 = (3.0 * cube - 6.0 * square + 4.0) / 6.0
        b2 = (-3.0 * cube + 3.0 * square + 3.0 * u + 1.0) / 6.0
        b3 = cube / 6.0
        knot = obs_knot[:, here]
        half = knot // HALF
        row = (obs_owner[:, here] * LIST + obs_slot[:, here]) * 2 + half
        chosen = hot(rows_a, row)
        sel[:, here] = chosen
        away = lax.broadcasted_iota(jnp.int32, (WIN, CHUNK), 0) - (knot - half * HALF)
        lin = jnp.where(
            away == 0,
            b0,
            jnp.where(
                away == 1, b1, jnp.where(away == 2, b2, jnp.where(away == 3, b3, F32(0.0)))
            ),
        )
        lin_all[:, here] = lin
        squares = lin * lin
        att = attitude_part[:, here]
        value = jnp.concatenate(
            [squares * (weighted * att[c : c + 1] * att[c : c + 1]) for c in range(4)], 0
        )
        high, low = split2(value)
        acc[...] += mm(high, chosen, NT) + mm(low, chosen, NT)
        unit = obs_calib[:, here]
        group = unit // share
        calibs = hot(LO, unit - group * share)
        calhot[:, here] = calibs
        part = calib_part[:, here]
        match = lax.broadcasted_iota(jnp.int32, (devices, CHUNK), 0) == group
        chigh, clow = split2(jnp.where(match, weighted * part * part, F32(0.0)))
        acc_cal[...] += mm(chigh, calibs, NT) + mm(clow, calibs, NT)
        return carry

    lax.fori_loop(0, count // CHUNK, diag_step, 0)
    send_diag[...] = packed(acc[...]).reshape(devices, 8, 4 * HALF)
    cdiag_keep[...] = acc_cal[...]

    pl.semaphore_wait(barrier, devices - 1)
    spread(send_diag, recv_diag, 0)

    all_sums = []
    for tile in range(tiles):
        here = pl.ds(tile * OBS_TILE, OBS_TILE)
        res = residual[:, here]
        parts = source_part[:, here]
        block = jnp.concatenate([parts, res, jnp.zeros((2, OBS_TILE), F32)], 0)
        weighted = weighted_all[:, here]
        columns = jnp.concatenate(
            [block * (weighted * parts[k : k + 1]) for k in range(5)]
            + [jnp.zeros((8, OBS_TILE), F32)],
            0,
        )
        stars = hot(SRC_TILE, obs_source[:, here])
        srchot[:, here] = stars
        high, middle, low = split3(columns)
        all_sums.append(mm(high, stars, NT) + (mm(middle, stars, NT) + mm(low, stars, NT)))
    sums = jnp.concatenate(all_sums, 1)
    matrix = [[sums[8 * min(l, r) + max(l, r)][None, :] for r in range(5)] for l in range(5)]
    target = [sums[8 * l + 5][None, :] for l in range(5)]
    for l in range(5):
        matrix[l][l] = matrix[l][l] + 1.0
    for pivot in range(5):
        for lower in range(pivot + 1, 5):
            factor = matrix[lower][pivot] / matrix[pivot][pivot]
            for r in range(pivot, 5):
                matrix[lower][r] = matrix[lower][r] - factor * matrix[pivot][r]
            target[lower] = target[lower] - factor * target[pivot]
    result = [None] * 5
    for pivot in range(4, -1, -1):
        value = target[pivot]
        for r in range(pivot + 1, 5):
            value = value - matrix[pivot][r] * result[r]
        result[pivot] = value / matrix[pivot][pivot]
    update = jnp.concatenate(result, 0)
    source_out[...] = update
    update8 = jnp.concatenate(result + [jnp.zeros((3, tiles * SRC_TILE), F32)], 0)
    uhigh, umiddle, ulow = split3(jnp.concatenate([update8, jnp.zeros_like(update8)], 0))
    for tile in range(tiles):
        here = pl.ds(tile * OBS_TILE, OBS_TILE)
        mine = slice(tile * SRC_TILE, (tile + 1) * SRC_TILE)
        stars = srchot[:, here]
        per_obs = mm(uhigh[:, mine], stars, NN) + (
            mm(umiddle[:, mine], stars, NN) + mm(ulow[:, mine], stars, NN)
        )
        first_all[:, here] = residual[:, here] - jnp.sum(
            source_part[:, here] * per_obs[0:5], axis=0, keepdims=True
        )

    acc[...] = jnp.zeros_like(acc)
    acc_cal[...] = jnp.zeros_like(acc_cal)

    def rhs_step(step, carry):
        here = pl.ds(pl.multiple_of(step * CHUNK, CHUNK), CHUNK)
        lin = lin_all[:, here]
        chosen = sel[:, here]
        scaled = weighted_all[:, here] * first_all[:, here]
        att = attitude_part[:, here]
        value = jnp.concatenate([lin * (scaled * att[c : c + 1]) for c in range(4)], 0)
        high, low = split2(value)
        acc[...] += mm(high, chosen, NT) + mm(low, chosen, NT)
        group = obs_calib[:, here] // share
        match = lax.broadcasted_iota(jnp.int32, (devices, CHUNK), 0) == group
        chigh, clow = split2(jnp.where(match, scaled * calib_part[:, here], F32(0.0)))
        calibs = calhot[:, here]
        acc_cal[...] += mm(chigh, calibs, NT) + mm(clow, calibs, NT)
        return carry

    lax.fori_loop(0, count // CHUNK, rhs_step, 0)
    send_rhs[...] = packed(acc[...]).reshape(devices, 8, 4 * HALF)
    spread(send_rhs, recv_rhs, 1)
    both = jnp.concatenate([acc_cal[...], cdiag_keep[...]], 1)
    send_cal[...] = both[:, None, :]
    spread(send_cal, recv_cal, 2)

    blocks = KB_DEV * 2
    wide = lax.broadcasted_iota(jnp.int32, (blocks, rows_a), 0)
    wide_half = lax.rem(lax.broadcasted_iota(jnp.int32, (blocks, rows_a), 1), 2)
    gather = jnp.where(wide == wide_half * KB_DEV + list_row[...], F32(1.0), F32(0.0)).astype(BF16)
    tall = lax.broadcasted_iota(jnp.int32, (rows_a, blocks), 1)
    tall_half = lax.rem(lax.broadcasted_iota(jnp.int32, (rows_a, blocks), 0), 2)
    scatter = jnp.where(tall == tall_half * KB_DEV + list_col[...], F32(1.0), F32(0.0)).astype(BF16)

    def owned(arrived):
        high, middle, low = split3(arrived[...].reshape(rows_a, 4 * HALF))
        return mm(gather, high, NN) + (mm(gather, middle, NN) + mm(gather, low, NN))

    arrive(recv_diag, 0)
    diag = owned(recv_diag)
    arrive(recv_rhs, 1)
    coef = owned(recv_rhs) / (diag + 1.0)
    high, middle, low = split3(coef)
    back = mm(scatter, high, NN) + (mm(scatter, middle, NN) + mm(scatter, low, NN))
    send_ret[...] = back.reshape(devices, 8, 4 * HALF)
    spread(send_ret, recv_ret, 3)
    arrive(recv_cal, 2)
    calsum = jnp.sum(recv_cal[...], axis=0)
    ratio = calsum / (pltpu.roll(calsum, LO, 1) + 1.0)
    send_calret[...] = ratio

    def one_cal(step, carry):
        _, where = peer_of(step)
        pltpu.make_async_remote_copy(
            src_ref=send_calret,
            dst_ref=recv_calret.at[me],
            send_sem=send_sem.at[4],
            recv_sem=recv_sem.at[4],
            device_id=where,
            device_id_type=pl.DeviceIdType.MESH,
        ).start()
        return carry

    pltpu.make_async_copy(send_calret, recv_calret.at[me], recv_sem.at[4]).start()
    lax.fori_loop(1, devices, one_cal, 0)
    for c in range(4):
        wide_rows = jnp.concatenate(
            [
                coef[0:KB_DEV, c * HALF : (c + 1) * HALF],
                coef[KB_DEV:blocks, c * HALF : (c + 1) * HALF],
            ],
            1,
        )
        for block in range(KB_DEV):
            attitude_out[c : c + 1, block * KNOT : (block + 1) * KNOT] = wide_rows[
                block : block + 1
            ]

    arrive(recv_calret, 4)
    calvals = recv_calret[...]
    calib_out[...] = calvals
    ctable = jnp.concatenate(split2(calvals.reshape(devices, 2 * LO)[:, 0:LO]), 0)
    arrive(recv_ret, 3)
    table = recv_ret[...].reshape(rows_a, 4 * HALF).T
    even = lax.rem(lax.broadcasted_iota(jnp.int32, (8, rows_a), 1), 2) == 0
    pieces = []
    for c in range(4):
        own = table[c * HALF : (c + 1) * HALF]
        pieces.append(own)
        pieces.append(jnp.where(even, pltpu.roll(own[0:8], rows_a - 1, 1), F32(0.0)))
    tables = jnp.concatenate(split2(jnp.concatenate(pieces, 0)), 0)
    acc_shape = 4 * WIN

    def correct_step(step, carry):
        here = pl.ds(pl.multiple_of(step * CHUNK, CHUNK), CHUNK)
        fetched = mm(tables, sel[:, here], NN)
        fetched = fetched[0:acc_shape] + fetched[acc_shape : 2 * acc_shape]
        att = attitude_part[:, here]
        projected = fetched[0:WIN] * att[0:1]
        for c in range(1, 4):
            projected = projected + fetched[c * WIN : (c + 1) * WIN] * att[c : c + 1]
        term = jnp.sum(projected * lin_all[:, here], axis=0, keepdims=True)
        group = obs_calib[:, here] // share
        match = lax.broadcasted_iota(jnp.int32, (devices, CHUNK), 0) == group
        cal = mm(ctable, calhot[:, here], NN)
        cal = jnp.where(match, cal[0:devices] + cal[devices : 2 * devices], F32(0.0))
        value = jnp.sum(cal, axis=0, keepdims=True)
        residual_out[:, here] = first_all[:, here] - term - calib_part[:, here] * value
        return carry

    lax.fori_loop(0, count // CHUNK, correct_step, 0)
    left(send_diag, 0)
    left(send_rhs, 1)
    left(send_cal, 2)
    left(send_ret, 3)
    part = recv_calret.at[pl.ds(0, devices - 1)]
    pltpu.make_async_copy(part, part, send_sem.at[4]).wait()


def on_device(n_src, n_att, *args):
    (
        residual,
        weight,
        source_part,
        attitude_part,
        calib_part,
        phase,
        obs_source,
        obs_owner,
        obs_slot,
        obs_knot,
        obs_calib,
        tile_count,
        time_list,
    ) = args
    devices = n_src * n_att
    count = residual.shape[0]
    sources = count // OBS_TILE * SRC_TILE
    rows_a = devices * LIST * 2
    listed = jnp.repeat(time_list.reshape(devices * LIST), 2)
    row = lambda x: x.reshape(1, count)
    vmem = pl.BlockSpec(memory_space=pltpu.VMEM)
    slab = pltpu.VMEM((devices, 8, 4 * HALF), F32)
    line = pltpu.VMEM((devices, 1, 2 * LO), F32)
    source_update, attitude_update, calib, residual_out = pl.pallas_call(
        functools.partial(kernel, devices, n_att),
        out_shape=(
            jax.ShapeDtypeStruct((5, sources), F32),
            jax.ShapeDtypeStruct((4, KB_DEV * KNOT), F32),
            jax.ShapeDtypeStruct((devices, 1, 2 * LO), F32),
            jax.ShapeDtypeStruct((1, count), F32),
        ),
        in_specs=[pl.BlockSpec(memory_space=pltpu.SMEM)] + [vmem] * 13,
        out_specs=(vmem,) * 4,
        scratch_shapes=[
            pltpu.VMEM((rows_a, count), BF16),
            pltpu.VMEM((WIN, count), F32),
            pltpu.VMEM((1, count), F32),
            pltpu.VMEM((1, count), F32),
            pltpu.VMEM((LO, count), BF16),
            pltpu.VMEM((SRC_TILE, count), BF16),
            pltpu.VMEM((4 * WIN, rows_a), F32),
            pltpu.VMEM((devices, LO), F32),
            pltpu.VMEM((devices, LO), F32),
            slab,
            slab,
            slab,
            slab,
            slab,
            slab,
            line,
            line,
            pltpu.VMEM((1, 2 * LO), F32),
            line,
            pltpu.SemaphoreType.DMA((5,)),
            pltpu.SemaphoreType.DMA((5,)),
        ],
        compiler_params=pltpu.CompilerParams(
            collective_id=0, has_side_effects=True, vmem_limit_bytes=56 * 1024 * 1024
        ),
    )(
        tile_count,
        row(residual),
        row(weight),
        source_part,
        attitude_part,
        row(calib_part),
        row(phase),
        row(obs_source),
        row(obs_owner),
        row(obs_slot),
        row(obs_knot),
        row(obs_calib),
        listed.reshape(1, rows_a),
        listed.reshape(rows_a, 1),
    )
    calib_update = calib[:, 0, 0 : NCAL // devices].reshape(NCAL)
    return source_update, attitude_update, calib_update, residual_out.reshape(count)


def solution(mesh):
    both = P(("src", "att"))
    columns = P(None, ("src", "att"))
    placed = (
        both,
        both,
        columns,
        columns,
        both,
        both,
        both,
        both,
        both,
        both,
        both,
        P(("src", "att"), None),
        P(None, ("src", "att"), None),
    )
    return jax.shard_map(
        functools.partial(on_device, mesh.shape["src"], mesh.shape["att"]),
        mesh=mesh,
        in_specs=placed,
        out_specs=(columns, columns, P(), both),
        check_vma=False,
    )
```

```python
import functools

import jax
import jax.numpy as jnp
from jax import lax
from jax.experimental import pallas as pl
from jax.experimental.pallas import tpu as pltpu
from jax.sharding import PartitionSpec as P

OBS_TILE = 2048
SRC_TILE = 64
KNOT = 128
LIST = 4
KB_DEV = 8
NCAL = 2048

HALF = 64
WIN = 72
LO = 64
CHUNK = 2048
F32 = jnp.float32
BF16 = jnp.bfloat16
NT = (((1,), (1,)), ((), ()))
NN = (((1,), (0,)), ((), ()))


def mm(left, right, dims):
    return lax.dot_general(left, right, dims, preferred_element_type=F32)


def split2(value):
    high = value.astype(BF16)
    low = (value - high.astype(F32)).astype(BF16)
    return high, low


def split3(value):
    high = value.astype(BF16)
    rest = value - high.astype(F32)
    middle = rest.astype(BF16)
    low = (rest - middle.astype(F32)).astype(BF16)
    return high, middle, low


def hot(rows, index):
    count = index.shape[1]
    match = lax.broadcasted_iota(jnp.int32, (rows, count), 0) == index
    return jnp.where(match, F32(1.0), F32(0.0)).astype(BF16)


def kernel(
    devices,
    n_att,
    count_ref,
    residual,
    weight,
    source_part,
    attitude_part,
    calib_part,
    phase,
    obs_source,
    obs_owner,
    obs_slot,
    obs_knot,
    obs_calib,
    listing,
    source_out,
    attitude_out,
    calib_out,
    residual_out,
    sel,
    lin_all,
    first_all,
    weighted_all,
    calhot,
    srchot,
    acc,
    acc_cal,
    cdiag_keep,
    send_diag,
    send_rhs,
    recv_diag,
    recv_rhs,
    send_ret,
    recv_ret,
    send_cal,
    recv_cal,
    send_calret,
    recv_calret,
    send_sem,
    recv_sem,
):
    rows_a = devices * LIST * 2
    count = residual.shape[1]
    tiles = count // OBS_TILE
    share = NCAL // devices
    me_src = lax.axis_index("src")
    me_att = lax.axis_index("att")
    me = me_src * n_att + me_att

    def peer_of(step):
        peer = lax.rem(me + step, devices)
        return peer, (peer // n_att, lax.rem(peer, n_att))

    barrier = pltpu.get_barrier_semaphore()

    def greet(step, carry):
        _, where = peer_of(step)
        pl.semaphore_signal(
            barrier, inc=1, device_id=where, device_id_type=pl.DeviceIdType.MESH
        )
        return carry

    lax.fori_loop(1, devices, greet, 0)

    def spread(source, target, which):
        def one(step, carry):
            peer, where = peer_of(step)
            pltpu.make_async_remote_copy(
                src_ref=source.at[peer],
                dst_ref=target.at[me],
                send_sem=send_sem.at[which],
                recv_sem=recv_sem.at[which],
                device_id=where,
                device_id_type=pl.DeviceIdType.MESH,
            ).start()
            return carry

        pltpu.make_async_copy(source.at[me], target.at[me], recv_sem.at[which]).start()
        lax.fori_loop(1, devices, one, 0)

    def arrive(target, which):
        pltpu.make_async_copy(target, target, recv_sem.at[which]).wait()

    def left(source, which):
        part = source.at[pl.ds(0, devices - 1)]
        pltpu.make_async_copy(part, part, send_sem.at[which]).wait()

    def packed(sums):
        odd = lax.rem(lax.broadcasted_iota(jnp.int32, (8, rows_a), 1), 2) == 1
        pieces = []
        for c in range(4):
            block = sums[c * WIN : (c + 1) * WIN]
            over = pltpu.roll(block[HALF:WIN], 1, 1)
            pieces.append(block[0:8] + jnp.where(odd, over, F32(0.0)))
            pieces.append(block[8:HALF])
        return jnp.concatenate(pieces, 0).T

    acc[...] = jnp.zeros_like(acc)
    acc_cal[...] = jnp.zeros_like(acc_cal)
    per_tile = OBS_TILE // CHUNK

    def diag_step(step, carry):
        here = pl.ds(pl.multiple_of(step * CHUNK, CHUNK), CHUNK)
        tile = step // per_tile
        place = lax.broadcasted_iota(jnp.int32, (1, CHUNK), 1) + (step - tile * per_tile) * CHUNK
        weighted = jnp.where(place < count_ref[0, tile], weight[:, here], F32(0.0))
        weighted_all[:, here] = weighted
        u = phase[:, here]
        other = 1.0 - u
        square = u * u
        cube = square * u
        b0 = other * other * other / 6.0
        b1 = (3.0 * cube - 6.0 * square + 4.0) / 6.0
        b2 = (-3.0 * cube + 3.0 * square + 3.0 * u + 1.0) / 6.0
        b3 = cube / 6.0
        knot = obs_knot[:, here]
        half = knot // HALF
        row = (obs_owner[:, here] * LIST + obs_slot[:, here]) * 2 + half
        chosen = hot(rows_a, row)
        sel[:, here] = chosen
        away = lax.broadcasted_iota(jnp.int32, (WIN, CHUNK), 0) - (knot - half * HALF)
        lin = jnp.where(
            away == 0,
            b0,
            jnp.where(
                away == 1, b1, jnp.where(away == 2, b2, jnp.where(away == 3, b3, F32(0.0)))
            ),
        )
        lin_all[:, here] = lin
        squares = lin * lin
        att = attitude_part[:, here]
        value = jnp.concatenate(
            [squares * (weighted * att[c : c + 1] * att[c : c + 1]) for c in range(4)], 0
        )
        high, low = split2(value)
        acc[...] += mm(high, chosen, NT) + mm(low, chosen, NT)
        unit = obs_calib[:, here]
        group = unit // share
        calibs = hot(LO, unit - group * share)
        calhot[:, here] = calibs
        part = calib_part[:, here]
        match = lax.broadcasted_iota(jnp.int32, (devices, CHUNK), 0) == group
        chigh, clow = split2(jnp.where(match, weighted * part * part, F32(0.0)))
        acc_cal[...] += mm(chigh, calibs, NT) + mm(clow, calibs, NT)
        return carry

    lax.fori_loop(0, count // CHUNK, diag_step, 0)
    send_diag[...] = packed(acc[...]).reshape(devices, 8, 4 * HALF)
    cdiag_keep[...] = acc_cal[...]

    blocks = KB_DEV * 2
    sender = lax.broadcasted_iota(jnp.int32, (rows_a, devices), 0) // (2 * LIST)
    sent = sender == lax.broadcasted_iota(jnp.int32, (rows_a, devices), 1)
    entries = mm(
        jnp.where(sent, F32(1.0), F32(0.0)).astype(BF16),
        listing[...].astype(F32).astype(BF16),
        NN,
    )
    slot = lax.rem(lax.broadcasted_iota(jnp.int32, (rows_a, LIST), 0) // 2, LIST)
    own_slot = slot == lax.broadcasted_iota(jnp.int32, (rows_a, LIST), 1)
    entry = jnp.sum(jnp.where(own_slot, entries, F32(0.0)), axis=1, keepdims=True)
    tall = lax.broadcasted_iota(jnp.int32, (rows_a, 128), 1)
    tall_half = lax.rem(lax.broadcasted_iota(jnp.int32, (rows_a, 128), 0), 2)
    named = (tall - tall_half * KB_DEV).astype(F32) == entry
    tall_hot = jnp.where(named, F32(1.0), F32(0.0))
    scatter = tall_hot[:, 0:blocks].astype(BF16)
    gather = tall_hot.T[0:blocks].astype(BF16)

    pl.semaphore_wait(barrier, devices - 1)
    spread(send_diag, recv_diag, 0)

    all_sums = []
    for tile in range(tiles):
        here = pl.ds(tile * OBS_TILE, OBS_TILE)
        res = residual[:, here]
        parts = source_part[:, here]
        block = jnp.concatenate([parts, res, jnp.zeros((2, OBS_TILE), F32)], 0)
        weighted = weighted_all[:, here]
        columns = jnp.concatenate(
            [block * (weighted * parts[k : k + 1]) for k in range(5)]
            + [jnp.zeros((8, OBS_TILE), F32)],
            0,
        )
        stars = hot(SRC_TILE, obs_source[:, here])
        srchot[:, here] = stars
        high, middle, low = split3(columns)
        all_sums.append(mm(high, stars, NT) + (mm(middle, stars, NT) + mm(low, stars, NT)))
    sums = jnp.concatenate(all_sums, 1)
    matrix = [[sums[8 * min(l, r) + max(l, r)][None, :] for r in range(5)] for l in range(5)]
    target = [sums[8 * l + 5][None, :] for l in range(5)]
    for l in range(5):
        matrix[l][l] = matrix[l][l] + 1.0
    for pivot in range(5):
        for lower in range(pivot + 1, 5):
            factor = matrix[lower][pivot] / matrix[pivot][pivot]
            for r in range(pivot, 5):
                matrix[lower][r] = matrix[lower][r] - factor * matrix[pivot][r]
            target[lower] = target[lower] - factor * target[pivot]
    result = [None] * 5
    for pivot in range(4, -1, -1):
        value = target[pivot]
        for r in range(pivot + 1, 5):
            value = value - matrix[pivot][r] * result[r]
        result[pivot] = value / matrix[pivot][pivot]
    update = jnp.concatenate(result, 0)
    source_out[...] = update
    update8 = jnp.concatenate(result + [jnp.zeros((3, tiles * SRC_TILE), F32)], 0)
    uhigh, umiddle, ulow = split3(jnp.concatenate([update8, jnp.zeros_like(update8)], 0))
    for tile in range(tiles):
        here = pl.ds(tile * OBS_TILE, OBS_TILE)
        mine = slice(tile * SRC_TILE, (tile + 1) * SRC_TILE)
        stars = srchot[:, here]
        per_obs = mm(uhigh[:, mine], stars, NN) + (
            mm(umiddle[:, mine], stars, NN) + mm(ulow[:, mine], stars, NN)
        )
        first_all[:, here] = residual[:, here] - jnp.sum(
            source_part[:, here] * per_obs[0:5], axis=0, keepdims=True
        )

    acc_cal[...] = jnp.zeros_like(acc_cal)

    def calib_step(step, carry):
        here = pl.ds(pl.multiple_of(step * CHUNK, CHUNK), CHUNK)
        scaled = weighted_all[:, here] * first_all[:, here]
        group = obs_calib[:, here] // share
        match = lax.broadcasted_iota(jnp.int32, (devices, CHUNK), 0) == group
        chigh, clow = split2(jnp.where(match, scaled * calib_part[:, here], F32(0.0)))
        calibs = calhot[:, here]
        acc_cal[...] += mm(chigh, calibs, NT) + mm(clow, calibs, NT)
        return carry

    lax.fori_loop(0, count // CHUNK, calib_step, 0)
    both = jnp.concatenate([acc_cal[...], cdiag_keep[...]], 1)
    send_cal[...] = both[:, None, :]
    spread(send_cal, recv_cal, 2)
    acc[...] = jnp.zeros_like(acc)

    def rhs_step(step, carry):
        here = pl.ds(pl.multiple_of(step * CHUNK, CHUNK), CHUNK)
        lin = lin_all[:, here]
        chosen = sel[:, here]
        scaled = weighted_all[:, here] * first_all[:, here]
        att = attitude_part[:, here]
        value = jnp.concatenate([lin * (scaled * att[c : c + 1]) for c in range(4)], 0)
        high, low = split2(value)
        acc[...] += mm(high, chosen, NT) + mm(low, chosen, NT)
        return carry

    lax.fori_loop(0, count // CHUNK, rhs_step, 0)
    send_rhs[...] = packed(acc[...]).reshape(devices, 8, 4 * HALF)
    spread(send_rhs, recv_rhs, 1)
    arrive(recv_cal, 2)
    calsum = jnp.sum(recv_cal[...], axis=0)
    ratio = calsum / (pltpu.roll(calsum, LO, 1) + 1.0)
    send_calret[...] = ratio

    def one_cal(step, carry):
        _, where = peer_of(step)
        pltpu.make_async_remote_copy(
            src_ref=send_calret,
            dst_ref=recv_calret.at[me],
            send_sem=send_sem.at[4],
            recv_sem=recv_sem.at[4],
            device_id=where,
            device_id_type=pl.DeviceIdType.MESH,
        ).start()
        return carry

    pltpu.make_async_copy(send_calret, recv_calret.at[me], recv_sem.at[4]).start()
    lax.fori_loop(1, devices, one_cal, 0)

    def owned(arrived):
        high, middle, low = split3(arrived[...].reshape(rows_a, 4 * HALF))
        return mm(gather, high, NN) + (mm(gather, middle, NN) + mm(gather, low, NN))

    arrive(recv_diag, 0)
    diag = owned(recv_diag)
    arrive(recv_rhs, 1)
    coef = owned(recv_rhs) / (diag + 1.0)
    high, middle, low = split3(coef)
    back = mm(scatter, high, NN) + (mm(scatter, middle, NN) + mm(scatter, low, NN))
    send_ret[...] = back.reshape(devices, 8, 4 * HALF)
    spread(send_ret, recv_ret, 3)
    for c in range(4):
        wide_rows = jnp.concatenate(
            [
                coef[0:KB_DEV, c * HALF : (c + 1) * HALF],
                coef[KB_DEV:blocks, c * HALF : (c + 1) * HALF],
            ],
            1,
        )
        for block in range(KB_DEV):
            attitude_out[c : c + 1, block * KNOT : (block + 1) * KNOT] = wide_rows[
                block : block + 1
            ]

    arrive(recv_calret, 4)
    calvals = recv_calret[...]
    per_row = 128 // share
    for block in range(NCAL // 128):
        calib_out[:, block * 128 : (block + 1) * 128] = jnp.concatenate(
            [calvals[block * per_row + k, :, 0:share] for k in range(per_row)], 1
        )
    ctable = jnp.concatenate(split2(calvals.reshape(devices, 2 * LO)[:, 0:LO]), 0)
    arrive(recv_ret, 3)
    table = recv_ret[...].reshape(rows_a, 4 * HALF).T
    even = lax.rem(lax.broadcasted_iota(jnp.int32, (8, rows_a), 1), 2) == 0
    pieces = []
    for c in range(4):
        own = table[c * HALF : (c + 1) * HALF]
        pieces.append(own)
        pieces.append(jnp.where(even, pltpu.roll(own[0:8], rows_a - 1, 1), F32(0.0)))
    tables = jnp.concatenate(split2(jnp.concatenate(pieces, 0)), 0)
    acc_shape = 4 * WIN

    def correct_step(step, carry):
        here = pl.ds(pl.multiple_of(step * CHUNK, CHUNK), CHUNK)
        fetched = mm(tables, sel[:, here], NN)
        fetched = fetched[0:acc_shape] + fetched[acc_shape : 2 * acc_shape]
        att = attitude_part[:, here]
        projected = fetched[0:WIN] * att[0:1]
        for c in range(1, 4):
            projected = projected + fetched[c * WIN : (c + 1) * WIN] * att[c : c + 1]
        term = jnp.sum(projected * lin_all[:, here], axis=0, keepdims=True)
        group = obs_calib[:, here] // share
        match = lax.broadcasted_iota(jnp.int32, (devices, CHUNK), 0) == group
        cal = mm(ctable, calhot[:, here], NN)
        cal = jnp.where(match, cal[0:devices] + cal[devices : 2 * devices], F32(0.0))
        value = jnp.sum(cal, axis=0, keepdims=True)
        residual_out[:, here] = first_all[:, here] - term - calib_part[:, here] * value
        return carry

    lax.fori_loop(0, count // CHUNK, correct_step, 0)
    left(send_diag, 0)
    left(send_rhs, 1)
    left(send_cal, 2)
    left(send_ret, 3)
    part = recv_calret.at[pl.ds(0, devices - 1)]
    pltpu.make_async_copy(part, part, send_sem.at[4]).wait()


def hand_over(*refs):
    for source, target in zip(refs[:4], refs[4:]):
        target[...] = source[...]


def on_device(n_src, n_att, *args):
    (
        residual,
        weight,
        source_part,
        attitude_part,
        calib_part,
        phase,
        obs_source,
        obs_owner,
        obs_slot,
        obs_knot,
        obs_calib,
        tile_count,
        time_list,
    ) = args
    devices = n_src * n_att
    count = residual.shape[0]
    sources = count // OBS_TILE * SRC_TILE
    rows_a = devices * LIST * 2
    row = lambda x: x.reshape(1, count)
    vmem = pl.BlockSpec(memory_space=pltpu.VMEM)
    slab = pltpu.VMEM((devices, 8, 4 * HALF), F32)
    line = pltpu.VMEM((devices, 1, 2 * LO), F32)
    results = pl.pallas_call(
        functools.partial(kernel, devices, n_att),
        out_shape=(
            jax.ShapeDtypeStruct((5, sources), F32),
            jax.ShapeDtypeStruct((4, KB_DEV * KNOT), F32),
            jax.ShapeDtypeStruct((1, NCAL), F32),
            jax.ShapeDtypeStruct((1, count), F32),
        ),
        in_specs=[pl.BlockSpec(memory_space=pltpu.SMEM)] + [vmem] * 12,
        out_specs=(vmem,) * 4,
        scratch_shapes=[
            pltpu.VMEM((rows_a, count), BF16),
            pltpu.VMEM((WIN, count), F32),
            pltpu.VMEM((1, count), F32),
            pltpu.VMEM((1, count), F32),
            pltpu.VMEM((LO, count), BF16),
            pltpu.VMEM((SRC_TILE, count), BF16),
            pltpu.VMEM((4 * WIN, rows_a), F32),
            pltpu.VMEM((devices, LO), F32),
            pltpu.VMEM((devices, LO), F32),
            slab,
            slab,
            slab,
            slab,
            slab,
            slab,
            line,
            line,
            pltpu.VMEM((1, 2 * LO), F32),
            line,
            pltpu.SemaphoreType.DMA((5,)),
            pltpu.SemaphoreType.DMA((5,)),
        ],
        compiler_params=pltpu.CompilerParams(
            collective_id=0, has_side_effects=True, vmem_limit_bytes=56 * 1024 * 1024
        ),
    )(
        tile_count,
        row(residual),
        row(weight),
        source_part,
        attitude_part,
        row(calib_part),
        row(phase),
        row(obs_source),
        row(obs_owner),
        row(obs_slot),
        row(obs_knot),
        row(obs_calib),
        time_list.reshape(devices, LIST),
    )
    source_update, attitude_update, calib_update, residual_out = pl.pallas_call(
        hand_over,
        out_shape=tuple(jax.ShapeDtypeStruct(r.shape, F32) for r in results),
        in_specs=[vmem] * 4,
        out_specs=(vmem,) * 4,
    )(*results)
    return source_update, attitude_update, calib_update.reshape(NCAL), residual_out.reshape(count)


def solution(mesh):
    both = P(("src", "att"))
    columns = P(None, ("src", "att"))
    placed = (
        both,
        both,
        columns,
        columns,
        both,
        both,
        both,
        both,
        both,
        both,
        both,
        P(("src", "att"), None),
        P(None, ("src", "att"), None),
    )
    return jax.shard_map(
        functools.partial(on_device, mesh.shape["src"], mesh.shape["att"]),
        mesh=mesh,
        in_specs=placed,
        out_specs=(columns, columns, P(), both),
        check_vma=False,
    )
```

```python
import functools

import jax
import jax.numpy as jnp
from jax import lax
from jax.experimental import pallas as pl
from jax.experimental.pallas import tpu as pltpu
from jax.sharding import PartitionSpec as P

OBS_TILE = 2048
SRC_TILE = 64
KNOT = 128
LIST = 4
KB_DEV = 8
NCAL = 2048

HALF = 64
WIN = 72
LO = 64
CHUNK = 2048
F32 = jnp.float32
BF16 = jnp.bfloat16
NT = (((1,), (1,)), ((), ()))
NN = (((1,), (0,)), ((), ()))


def mm(left, right, dims):
    return lax.dot_general(left, right, dims, preferred_element_type=F32)


def split2(value):
    high = value.astype(BF16)
    low = (value - high.astype(F32)).astype(BF16)
    return high, low


def split3(value):
    high = value.astype(BF16)
    rest = value - high.astype(F32)
    middle = rest.astype(BF16)
    low = (rest - middle.astype(F32)).astype(BF16)
    return high, middle, low


def hot(rows, index):
    count = index.shape[1]
    match = lax.broadcasted_iota(jnp.int32, (rows, count), 0) == index
    return jnp.where(match, F32(1.0), F32(0.0)).astype(BF16)


def kernel(
    devices,
    n_att,
    count_ref,
    residual,
    weight,
    source_part,
    attitude_part,
    calib_part,
    phase,
    obs_source,
    obs_owner,
    obs_slot,
    obs_knot,
    obs_calib,
    listing,
    source_out,
    attitude_out,
    calib_out,
    residual_out,
    sel,
    lin_all,
    first_all,
    weighted_all,
    calhot,
    srchot,
    acc,
    acc_cal,
    cdiag_keep,
    send_diag,
    send_rhs,
    recv_diag,
    recv_rhs,
    send_ret,
    recv_ret,
    send_cal,
    recv_cal,
    send_calret,
    recv_calret,
    send_sem,
    recv_sem,
):
    rows_a = devices * LIST * 2
    count = residual.shape[1]
    tiles = count // OBS_TILE
    share = NCAL // devices
    me_src = lax.axis_index("src")
    me_att = lax.axis_index("att")
    me = me_src * n_att + me_att

    def peer_of(step):
        peer = lax.rem(me + step, devices)
        return peer, (peer // n_att, lax.rem(peer, n_att))

    barrier = pltpu.get_barrier_semaphore()

    def greet(step, carry):
        _, where = peer_of(step)
        pl.semaphore_signal(
            barrier, inc=1, device_id=where, device_id_type=pl.DeviceIdType.MESH
        )
        return carry

    lax.fori_loop(1, devices, greet, 0, unroll=True)

    def spread(source, target, which):
        def one(step, carry):
            peer, where = peer_of(step)
            pltpu.make_async_remote_copy(
                src_ref=source.at[peer],
                dst_ref=target.at[me],
                send_sem=send_sem.at[which],
                recv_sem=recv_sem.at[which],
                device_id=where,
                device_id_type=pl.DeviceIdType.MESH,
            ).start()
            return carry

        pltpu.make_async_copy(source.at[me], target.at[me], recv_sem.at[which]).start()
        lax.fori_loop(1, devices, one, 0, unroll=True)

    def arrive(target, which):
        pltpu.make_async_copy(target, target, recv_sem.at[which]).wait()

    def left(source, which):
        part = source.at[pl.ds(0, devices - 1)]
        pltpu.make_async_copy(part, part, send_sem.at[which]).wait()

    def packed(sums):
        odd = lax.rem(lax.broadcasted_iota(jnp.int32, (8, rows_a), 1), 2) == 1
        pieces = []
        for c in range(4):
            block = sums[c * WIN : (c + 1) * WIN]
            over = pltpu.roll(block[HALF:WIN], 1, 1)
            pieces.append(block[0:8] + jnp.where(odd, over, F32(0.0)))
            pieces.append(block[8:HALF])
        return jnp.concatenate(pieces, 0).T

    acc[...] = jnp.zeros_like(acc)
    acc_cal[...] = jnp.zeros_like(acc_cal)
    per_tile = OBS_TILE // CHUNK

    def diag_step(step, carry):
        here = pl.ds(pl.multiple_of(step * CHUNK, CHUNK), CHUNK)
        tile = step // per_tile
        place = lax.broadcasted_iota(jnp.int32, (1, CHUNK), 1) + (step - tile * per_tile) * CHUNK
        weighted = jnp.where(place < count_ref[0, tile], weight[:, here], F32(0.0))
        weighted_all[:, here] = weighted
        u = phase[:, here]
        other = 1.0 - u
        square = u * u
        cube = square * u
        b0 = other * other * other / 6.0
        b1 = (3.0 * cube - 6.0 * square + 4.0) / 6.0
        b2 = (-3.0 * cube + 3.0 * square + 3.0 * u + 1.0) / 6.0
        b3 = cube / 6.0
        knot = obs_knot[:, here]
        half = knot // HALF
        row = (obs_owner[:, here] * LIST + obs_slot[:, here]) * 2 + half
        chosen = hot(rows_a, row)
        sel[:, here] = chosen
        away = lax.broadcasted_iota(jnp.int32, (WIN, CHUNK), 0) - (knot - half * HALF)
        lin = jnp.where(
            away == 0,
            b0,
            jnp.where(
                away == 1, b1, jnp.where(away == 2, b2, jnp.where(away == 3, b3, F32(0.0)))
            ),
        )
        lin_all[:, here] = lin
        squares = lin * lin
        att = attitude_part[:, here]
        value = jnp.concatenate(
            [squares * (weighted * att[c : c + 1] * att[c : c + 1]) for c in range(4)], 0
        )
        high, low = split2(value)
        acc[...] += mm(high, chosen, NT) + mm(low, chosen, NT)
        unit = obs_calib[:, here]
        group = unit // share
        calibs = hot(LO, unit - group * share)
        calhot[:, here] = calibs
        part = calib_part[:, here]
        match = lax.broadcasted_iota(jnp.int32, (devices, CHUNK), 0) == group
        chigh, clow = split2(jnp.where(match, weighted * part * part, F32(0.0)))
        acc_cal[...] += mm(chigh, calibs, NT) + mm(clow, calibs, NT)
        return carry

    lax.fori_loop(0, count // CHUNK, diag_step, 0)
    send_diag[...] = packed(acc[...]).reshape(devices, 8, 4 * HALF)
    cdiag_keep[...] = acc_cal[...]

    blocks = KB_DEV * 2
    sender = lax.broadcasted_iota(jnp.int32, (rows_a, devices), 0) // (2 * LIST)
    sent = sender == lax.broadcasted_iota(jnp.int32, (rows_a, devices), 1)
    entries = mm(
        jnp.where(sent, F32(1.0), F32(0.0)).astype(BF16),
        listing[:, 0, :].astype(F32).astype(BF16),
        NN,
    )
    slot = lax.rem(lax.broadcasted_iota(jnp.int32, (rows_a, LIST), 0) // 2, LIST)
    own_slot = slot == lax.broadcasted_iota(jnp.int32, (rows_a, LIST), 1)
    entry = jnp.sum(jnp.where(own_slot, entries, F32(0.0)), axis=1, keepdims=True)
    tall = lax.broadcasted_iota(jnp.int32, (rows_a, 128), 1)
    tall_half = lax.rem(lax.broadcasted_iota(jnp.int32, (rows_a, 128), 0), 2)
    named = (tall - tall_half * KB_DEV).astype(F32) == entry
    tall_hot = jnp.where(named, F32(1.0), F32(0.0))
    scatter = tall_hot[:, 0:blocks].astype(BF16)
    gather = tall_hot.T[0:blocks].astype(BF16)

    pl.semaphore_wait(barrier, devices - 1)
    spread(send_diag, recv_diag, 0)

    all_sums = []
    for tile in range(tiles):
        here = pl.ds(tile * OBS_TILE, OBS_TILE)
        res = residual[:, here]
        parts = source_part[:, here]
        block = jnp.concatenate([parts, res, jnp.zeros((2, OBS_TILE), F32)], 0)
        weighted = weighted_all[:, here]
        columns = jnp.concatenate(
            [block * (weighted * parts[k : k + 1]) for k in range(5)]
            + [jnp.zeros((8, OBS_TILE), F32)],
            0,
        )
        stars = hot(SRC_TILE, obs_source[:, here])
        srchot[:, here] = stars
        high, middle, low = split3(columns)
        all_sums.append(mm(high, stars, NT) + (mm(middle, stars, NT) + mm(low, stars, NT)))
    sums = jnp.concatenate(all_sums, 1)
    matrix = [[sums[8 * min(l, r) + max(l, r)][None, :] for r in range(5)] for l in range(5)]
    target = [sums[8 * l + 5][None, :] for l in range(5)]
    for l in range(5):
        matrix[l][l] = matrix[l][l] + 1.0
    for pivot in range(5):
        for lower in range(pivot + 1, 5):
            factor = matrix[lower][pivot] / matrix[pivot][pivot]
            for r in range(pivot, 5):
                matrix[lower][r] = matrix[lower][r] - factor * matrix[pivot][r]
            target[lower] = target[lower] - factor * target[pivot]
    result = [None] * 5
    for pivot in range(4, -1, -1):
        value = target[pivot]
        for r in range(pivot + 1, 5):
            value = value - matrix[pivot][r] * result[r]
        result[pivot] = value / matrix[pivot][pivot]
    update = jnp.concatenate(result, 0)
    source_out[...] = update
    update8 = jnp.concatenate(result + [jnp.zeros((3, tiles * SRC_TILE), F32)], 0)
    uhigh, umiddle, ulow = split3(jnp.concatenate([update8, jnp.zeros_like(update8)], 0))
    for tile in range(tiles):
        here = pl.ds(tile * OBS_TILE, OBS_TILE)
        mine = slice(tile * SRC_TILE, (tile + 1) * SRC_TILE)
        stars = srchot[:, here]
        per_obs = mm(uhigh[:, mine], stars, NN) + (
            mm(umiddle[:, mine], stars, NN) + mm(ulow[:, mine], stars, NN)
        )
        first_all[:, here] = residual[:, here] - jnp.sum(
            source_part[:, here] * per_obs[0:5], axis=0, keepdims=True
        )

    acc_cal[...] = jnp.zeros_like(acc_cal)

    def calib_step(step, carry):
        here = pl.ds(pl.multiple_of(step * CHUNK, CHUNK), CHUNK)
        scaled = weighted_all[:, here] * first_all[:, here]
        group = obs_calib[:, here] // share
        match = lax.broadcasted_iota(jnp.int32, (devices, CHUNK), 0) == group
        chigh, clow = split2(jnp.where(match, scaled * calib_part[:, here], F32(0.0)))
        calibs = calhot[:, here]
        acc_cal[...] += mm(chigh, calibs, NT) + mm(clow, calibs, NT)
        return carry

    lax.fori_loop(0, count // CHUNK, calib_step, 0)
    both = jnp.concatenate([acc_cal[...], cdiag_keep[...]], 1)
    send_cal[...] = both[:, None, :]
    spread(send_cal, recv_cal, 2)
    acc[...] = jnp.zeros_like(acc)

    def rhs_step(step, carry):
        here = pl.ds(pl.multiple_of(step * CHUNK, CHUNK), CHUNK)
        lin = lin_all[:, here]
        chosen = sel[:, here]
        scaled = weighted_all[:, here] * first_all[:, here]
        att = attitude_part[:, here]
        value = jnp.concatenate([lin * (scaled * att[c : c + 1]) for c in range(4)], 0)
        high, low = split2(value)
        acc[...] += mm(high, chosen, NT) + mm(low, chosen, NT)
        return carry

    lax.fori_loop(0, count // CHUNK, rhs_step, 0)
    send_rhs[...] = packed(acc[...]).reshape(devices, 8, 4 * HALF)
    spread(send_rhs, recv_rhs, 1)
    arrive(recv_cal, 2)
    calsum = jnp.sum(recv_cal[...], axis=0)
    ratio = calsum / (pltpu.roll(calsum, LO, 1) + 1.0)
    send_calret[...] = ratio

    def one_cal(step, carry):
        _, where = peer_of(step)
        pltpu.make_async_remote_copy(
            src_ref=send_calret,
            dst_ref=recv_calret.at[me],
            send_sem=send_sem.at[4],
            recv_sem=recv_sem.at[4],
            device_id=where,
            device_id_type=pl.DeviceIdType.MESH,
        ).start()
        return carry

    pltpu.make_async_copy(send_calret, recv_calret.at[me], recv_sem.at[4]).start()
    lax.fori_loop(1, devices, one_cal, 0, unroll=True)

    def owned(arrived):
        high, middle, low = split3(arrived[...].reshape(rows_a, 4 * HALF))
        return mm(gather, high, NN) + (mm(gather, middle, NN) + mm(gather, low, NN))

    arrive(recv_diag, 0)
    diag = owned(recv_diag)
    arrive(recv_rhs, 1)
    coef = owned(recv_rhs) / (diag + 1.0)
    high, middle, low = split3(coef)
    back = mm(scatter, high, NN) + (mm(scatter, middle, NN) + mm(scatter, low, NN))
    send_ret[...] = back.reshape(devices, 8, 4 * HALF)
    spread(send_ret, recv_ret, 3)
    for c in range(4):
        wide_rows = jnp.concatenate(
            [
                coef[0:KB_DEV, c * HALF : (c + 1) * HALF],
                coef[KB_DEV:blocks, c * HALF : (c + 1) * HALF],
            ],
            1,
        )
        for block in range(KB_DEV):
            attitude_out[c : c + 1, block * KNOT : (block + 1) * KNOT] = wide_rows[
                block : block + 1
            ]

    arrive(recv_calret, 4)
    calvals = recv_calret[...]
    per_row = 128 // share
    for block in range(NCAL // 128):
        calib_out[:, block * 128 : (block + 1) * 128] = jnp.concatenate(
            [calvals[block * per_row + k, :, 0:share] for k in range(per_row)], 1
        )
    ctable = jnp.concatenate(split2(calvals.reshape(devices, 2 * LO)[:, 0:LO]), 0)
    arrive(recv_ret, 3)
    table = recv_ret[...].reshape(rows_a, 4 * HALF).T
    even = lax.rem(lax.broadcasted_iota(jnp.int32, (8, rows_a), 1), 2) == 0
    pieces = []
    for c in range(4):
        own = table[c * HALF : (c + 1) * HALF]
        pieces.append(own)
        pieces.append(jnp.where(even, pltpu.roll(own[0:8], rows_a - 1, 1), F32(0.0)))
    tables = jnp.concatenate(split2(jnp.concatenate(pieces, 0)), 0)
    acc_shape = 4 * WIN

    def correct_step(step, carry):
        here = pl.ds(pl.multiple_of(step * CHUNK, CHUNK), CHUNK)
        fetched = mm(tables, sel[:, here], NN)
        fetched = fetched[0:acc_shape] + fetched[acc_shape : 2 * acc_shape]
        att = attitude_part[:, here]
        projected = fetched[0:WIN] * att[0:1]
        for c in range(1, 4):
            projected = projected + fetched[c * WIN : (c + 1) * WIN] * att[c : c + 1]
        term = jnp.sum(projected * lin_all[:, here], axis=0, keepdims=True)
        group = obs_calib[:, here] // share
        match = lax.broadcasted_iota(jnp.int32, (devices, CHUNK), 0) == group
        cal = mm(ctable, calhot[:, here], NN)
        cal = jnp.where(match, cal[0:devices] + cal[devices : 2 * devices], F32(0.0))
        value = jnp.sum(cal, axis=0, keepdims=True)
        residual_out[:, here] = first_all[:, here] - term - calib_part[:, here] * value
        return carry

    lax.fori_loop(0, count // CHUNK, correct_step, 0)
    left(send_diag, 0)
    left(send_rhs, 1)
    left(send_cal, 2)
    left(send_ret, 3)
    part = recv_calret.at[pl.ds(0, devices - 1)]
    pltpu.make_async_copy(part, part, send_sem.at[4]).wait()


def hand_over(*refs):
    for source, target in zip(refs[:4], refs[4:]):
        target[...] = source[...]


def on_device(n_src, n_att, *args):
    (
        residual,
        weight,
        source_part,
        attitude_part,
        calib_part,
        phase,
        obs_source,
        obs_owner,
        obs_slot,
        obs_knot,
        obs_calib,
        tile_count,
        time_list,
    ) = args
    devices = n_src * n_att
    count = residual.shape[0]
    sources = count // OBS_TILE * SRC_TILE
    rows_a = devices * LIST * 2
    row = lambda x: x.reshape(1, count)
    vmem = pl.BlockSpec(memory_space=pltpu.VMEM)
    slab = pltpu.VMEM((devices, 8, 4 * HALF), F32)
    line = pltpu.VMEM((devices, 1, 2 * LO), F32)
    results = pl.pallas_call(
        functools.partial(kernel, devices, n_att),
        out_shape=(
            jax.ShapeDtypeStruct((5, sources), F32),
            jax.ShapeDtypeStruct((4, KB_DEV * KNOT), F32),
            jax.ShapeDtypeStruct((1, NCAL), F32),
            jax.ShapeDtypeStruct((1, count), F32),
        ),
        in_specs=[pl.BlockSpec(memory_space=pltpu.SMEM)] + [vmem] * 12,
        out_specs=(vmem,) * 4,
        scratch_shapes=[
            pltpu.VMEM((rows_a, count), BF16),
            pltpu.VMEM((WIN, count), F32),
            pltpu.VMEM((1, count), F32),
            pltpu.VMEM((1, count), F32),
            pltpu.VMEM((LO, count), BF16),
            pltpu.VMEM((SRC_TILE, count), BF16),
            pltpu.VMEM((4 * WIN, rows_a), F32),
            pltpu.VMEM((devices, LO), F32),
            pltpu.VMEM((devices, LO), F32),
            slab,
            slab,
            slab,
            slab,
            slab,
            slab,
            line,
            line,
            pltpu.VMEM((1, 2 * LO), F32),
            line,
            pltpu.SemaphoreType.DMA((5,)),
            pltpu.SemaphoreType.DMA((5,)),
        ],
        compiler_params=pltpu.CompilerParams(
            collective_id=0, has_side_effects=True, vmem_limit_bytes=56 * 1024 * 1024
        ),
    )(
        tile_count,
        row(residual),
        row(weight),
        source_part,
        attitude_part,
        row(calib_part),
        row(phase),
        row(obs_source),
        row(obs_owner),
        row(obs_slot),
        row(obs_knot),
        row(obs_calib),
        time_list,
    )
    source_update, attitude_update, calib_update, residual_out = pl.pallas_call(
        hand_over,
        out_shape=tuple(jax.ShapeDtypeStruct(r.shape, F32) for r in results),
        in_specs=[vmem] * 4,
        out_specs=(vmem,) * 4,
    )(*results)
    return source_update, attitude_update, calib_update.reshape(NCAL), residual_out.reshape(count)


def solution(mesh):
    both = P(("src", "att"))
    columns = P(None, ("src", "att"))
    placed = (
        both,
        both,
        columns,
        columns,
        both,
        both,
        both,
        both,
        both,
        both,
        both,
        P(("src", "att"), None),
        P(None, ("src", "att"), None),
    )
    return jax.shard_map(
        functools.partial(on_device, mesh.shape["src"], mesh.shape["att"]),
        mesh=mesh,
        in_specs=placed,
        out_specs=(columns, columns, P(), both),
        check_vma=False,
    )
```
